32 devices in a mesh: blk: 2 (over x), team: 16 (over z, y, core).
Axes of the slice: x: 2, y: 2, z: 4, core: 2. Of those that a mesh axis runs over, the one named last changes fastest.
Arguments:
- queries: bfloat16 [2, 1024, 512], P('blk', 'team'), may hold values from -6 to 6
- keys: bfloat16 [2, 16, 256, 512], P('blk', 'team'), may hold values from -6 to 6
- values: bfloat16 [2, 16, 256, 512], P('blk', 'team'), may hold values from -40 to 40
- block_ids: int32 [2, 16, 8, 2], P('blk', 'team'), may hold values from 0 to 3, as said below
- masks: int32 [2, 16, 8, 2, 16, 128], P('blk', 'team'), may hold values from 0 to 255
- gate_input: bfloat16 [2, 1024, 512], P('blk', 'team'), may hold values from -6 to 6
- w_gate: bfloat16 [512, 512], replicated, may hold values from -0.25 to 0.25
Outputs:
- gated: bfloat16 [2, 1024, 512], P('blk', 'team')
The draws below stay inside these ranges and needn't reach their ends.
Inputs may be any that keep to these rules, and one draw needn't show every extreme that they name: `block_ids`: each query tile lists 2 distinct blocks of its team; block c is 128 rows starting at (c % 2) * 128 of the key owner c // 2 along blk in the same team. Bit i of masks[g, t, q, j, w, a] is the mask between query row a of tile q and key row 8 w + i of listed block j.
All inputs are finite; a program needn't handle non-finite values.
Results may differ from the reference program's by a relative error of at most 0.0049.
Values may be sent and summed in bfloat16 or wider, within the bound.
A program may use at most 64 MiB of HBM per device.

```python
import math
import jax
import jax.numpy as jnp
from jax import lax

F = 512
TILE = 128
QT = 8
KB = 2
NB = 2
QG = 1024
KV_DEV = 256
WORDS = 16
N_BLK = 2
N_TEAM = 16


def draw_block_ids(key, part):
    lists = N_BLK * N_TEAM * QT
    list_keys = jax.random.split(key, lists)

    def draw_list(list_key):
        return jax.random.permutation(list_key, N_BLK * KB)[:NB].astype(jnp.int32)
    return jax.vmap(draw_list)(list_keys).reshape(N_BLK, N_TEAM, QT, NB)


def draw_values(key, part):
    key_cols, key_base = jax.random.split(key, 2)
    full_shape = (N_BLK, N_TEAM, KV_DEV, F)
    col_scale = jnp.exp(jax.random.uniform(key_cols, (F,), jnp.float32) * math.log(10.0))
    base_draw = jnp.clip(jax.random.normal(key_base, full_shape, jnp.float32), -4.0, 4.0)
    return (base_draw * col_scale).astype(jnp.bfloat16)


def with_ends(result, rng, low, largest):
    spot = [jax.random.randint(jax.random.fold_in(rng, axis), (), 0, length) for axis, length in enumerate(result.shape)]
    widest = result.shape.index(max(result.shape))
    next_to = spot[:widest] + [(spot[widest] + 1) % result.shape[widest]] + spot[widest + 1:]
    return result.at[tuple(spot)].set(low).at[tuple(next_to)].set(largest)


def steps_of(own_key, extent, cuts, low, largest):
    gain, own = 1.0, jax.random.fold_in(own_key, 6)
    for axis_at, blocks in cuts:
        draws = jnp.exp(jax.random.uniform(jax.random.fold_in(own, axis_at), (blocks,), jnp.float32, low / len(cuts), largest / len(cuts)))
        gain = gain * jnp.repeat(draws, extent[axis_at] // blocks).reshape([-1 if axis == axis_at else 1 for axis in range(len(extent))])
    return gain


def scatter_about(stream_key, shape, deviation, limit, shards=(), held_as=jnp.bfloat16):
    values = jax.random.normal(stream_key, shape, jnp.float32) * deviation
    if len(shards) > 0:
        values = steps_of(stream_key, shape, shards, -0.22, 0.18) * values
    return jnp.clip(values, min=-limit, max=limit).astype(held_as)


def setup_inputs(seed: int = 0) -> dict:
    key_list = jax.random.split(jax.random.key(seed), 8)
    queries = scatter_about(key_list[0], (N_BLK, QG, F), 1.0, 6.0, ((0, 2), (1, 16)))
    keys = scatter_about(key_list[1], (N_BLK, N_TEAM, KV_DEV, F), 1.0, 6.0, ((0, 2), (1, 16)))
    values = draw_values(jax.random.fold_in(key_list[7], 71), 0)
    block_ids = draw_block_ids(jax.random.fold_in(key_list[7], 71), 0)
    masks = with_ends(jax.random.randint(key_list[4], (N_BLK, N_TEAM, QT, NB, WORDS, TILE), 0, 256), jax.random.fold_in(key_list[4], 1), 0, 255).astype(jnp.int32)
    gate_input = scatter_about(key_list[5], (N_BLK, QG, F), 1.0, 6.0, ((0, 2), (1, 16)))
    w_gate = scatter_about(key_list[6], (F, F), F ** -0.5, 0.25)
    return dict(queries=queries, keys=keys, values=values, block_ids=block_ids, masks=masks, gate_input=gate_input, w_gate=w_gate)


def unpack(packed):
    shifts = jnp.arange(8, dtype=jnp.int32)
    mask_bits = jnp.bitwise_and(jnp.right_shift(packed[..., :, None, :], shifts[:, None]), 1)
    return mask_bits.reshape(packed.shape[:-2] + (packed.shape[-2] * 8, packed.shape[-1]))

def reference(queries, keys, values, block_ids, masks, gate_input, w_gate):
    score_scale = 1.0 / math.sqrt(F)
    highest = lax.Precision.HIGHEST

    def group(group_index):
        query_tiles = queries[group_index].reshape(QT, TILE, F).astype(jnp.float32)

        def team_step(totals, team_index):
            key_blocks = keys[:, team_index].reshape(N_BLK * KB, TILE, F)
            value_blocks = values[:, team_index].reshape(N_BLK * KB, TILE, F)
            block_list = block_ids[group_index, team_index]
            key_tiles = key_blocks[block_list].astype(jnp.float32)
            value_tiles = value_blocks[block_list].astype(jnp.float32)
            scores = jnp.einsum('qjbf,qaf->qjba', key_tiles, query_tiles, precision=highest) * score_scale
            mask_bits = unpack(masks[group_index, team_index]).astype(jnp.float32)
            weights = (mask_bits * jax.nn.sigmoid(scores)).astype(jnp.bfloat16)
            weights = lax.optimization_barrier(weights).astype(jnp.float32)
            added = jnp.einsum('qjba,qjbf->qaf', weights, value_tiles, precision=highest)
            return (totals + added, None)
        totals, _ = lax.scan(team_step, jnp.zeros((QT, TILE, F), jnp.float32), jnp.arange(N_TEAM, dtype=jnp.int32))
        aggregate = totals.reshape(QT * TILE, F)
        gate_pre = jnp.dot(gate_input[group_index], w_gate, preferred_element_type=jnp.float32)
        normed = aggregate * lax.rsqrt(lax.optimization_barrier(jnp.mean(aggregate * aggregate, axis=-1, keepdims=True)) + 1e-06)
        return (jax.nn.silu(gate_pre) * normed).astype(jnp.bfloat16)
    return lax.map(group, jnp.arange(N_BLK, dtype=jnp.int32))
```

```python
import functools
import math

import jax
import jax.numpy as jnp
from jax import lax
from jax.experimental import pallas as pl
from jax.experimental.pallas import tpu as pltpu
from jax.sharding import PartitionSpec as P

MESH = pl.DeviceIdType.MESH


def kernel(
    n_blk, n_team, n_lo, n_mid, n_hi, n_chunk,
    ids_ref, q_ref, k_ref, v_ref, mask_ref, gate_in_ref, w_gate_ref,
    out_ref,
    qbuf, kbuf, vbuf, wbuf, gate_buf, total,
    keep1, s1_send, s1_recv, keep2, s2_send, s2_recv, s3_send, s3_recv,
    loc_sem,
    kv_send, kv_recv,
    zq_send, zq_recv, yq_send, yq_recv, cq_send, cq_recv,
    r1_send, r1_recv, r2_send, r2_recv, r3_send, r3_recv,
):
    rows, width = q_ref.shape
    kv_rows = k_ref.shape[0]
    tiles, slots, words, tile_rows = mask_ref.shape
    key_blocks = kv_rows // tile_rows
    cw = width // n_chunk
    scale = 1.0 / math.sqrt(width)

    blk = lax.axis_index("blk")
    team = lax.axis_index("team")
    lo = lax.rem(team, n_lo)
    mid = lax.rem(team // n_lo, n_mid)
    hi = team // (n_lo * n_mid)

    def index_of(h, m, l):
        return (h * n_mid + m) * n_lo + l

    core_peer = (blk, index_of(hi, mid, 1 - lo))
    mid_peer = (blk, index_of(hi, 1 - mid, lo))
    hi_to = [(blk, index_of(lax.rem(hi + s, n_hi), mid, lo)) for s in range(n_hi)]
    hi_from = [lax.rem(hi + n_hi - s, n_hi) for s in range(n_hi)]
    blk_to = [(lax.rem(blk + s, n_blk), team) for s in range(n_blk)]
    blk_from = [lax.rem(blk + n_blk - s, n_blk) for s in range(n_blk)]

    def remote(src, dst, send, recv, device):
        return pltpu.make_async_remote_copy(
            src_ref=src, dst_ref=dst, send_sem=send, recv_sem=recv,
            device_id=device, device_id_type=MESH,
        )

    locals_ = [
        pltpu.make_async_copy(q_ref, qbuf.at[team], loc_sem.at[0]),
        pltpu.make_async_copy(k_ref, kbuf.at[blk], loc_sem.at[1]),
    ]
    for c in range(n_chunk):
        locals_.append(
            pltpu.make_async_copy(
                v_ref.at[:, pl.ds(c * cw, cw)], vbuf.at[c, blk], loc_sem.at[2 + c]
            )
        )
    for copy in locals_:
        copy.start()

    barrier = pltpu.get_barrier_semaphore()
    partners = [core_peer, mid_peer] + hi_to[1:] + blk_to[1:]
    for device in partners:
        pl.semaphore_signal(barrier, inc=1, device_id=device, device_id_type=MESH)
    pl.semaphore_wait(barrier, len(partners))

    pending = []

    def start(copy):
        copy.start()
        pending.append(copy)
        return copy

    zq = [None] + [
        start(remote(q_ref, qbuf.at[team], zq_send.at[s], zq_recv.at[s], hi_to[s]))
        for s in range(1, n_hi)
    ]
    yq = [start(remote(q_ref, qbuf.at[team], yq_send.at[0], yq_recv.at[0], mid_peer))]
    k_copies = [None] + [
        start(remote(k_ref, kbuf.at[blk], kv_send.at[0, s], kv_recv.at[0, s], blk_to[s]))
        for s in range(1, n_blk)
    ]
    cq = [start(remote(q_ref, qbuf.at[team], cq_send.at[0, 0], cq_recv.at[0, 0], core_peer))]
    v_copies = []
    for c in range(n_chunk):
        v_copies.append(
            [None] + [
                start(
                    remote(
                        v_ref.at[:, pl.ds(c * cw, cw)], vbuf.at[c, blk],
                        kv_send.at[1 + c, s], kv_recv.at[1 + c, s], blk_to[s],
                    )
                )
                for s in range(1, n_blk)
            ]
        )

    for s in range(1, n_hi):
        zq[s].wait_recv()
        shard = qbuf.at[index_of(hi_from[s], mid, lo)]
        yq.append(start(remote(shard, shard, yq_send.at[s], yq_recv.at[s], mid_peer)))
        cq.append(start(remote(shard, shard, cq_send.at[0, s], cq_recv.at[0, s], core_peer)))

    gate_pre = jnp.dot(gate_in_ref[...], w_gate_ref[...], preferred_element_type=jnp.float32)
    gate_buf[...] = gate_pre / (1.0 + jnp.exp(-gate_pre))

    for s in range(n_hi):
        yq[s].wait_recv()
        shard = qbuf.at[index_of(hi_from[s], 1 - mid, lo)]
        cq.append(start(remote(shard, shard, cq_send.at[1, s], cq_recv.at[1, s], core_peer)))
    for copy in locals_:
        copy.wait()
    for copy in cq:
        copy.wait_recv()
    for copy in k_copies[1:]:
        copy.wait_recv()

    devices_per_tile = tile_rows // rows
    shifts = lax.broadcasted_iota(jnp.int32, (words, 8, tile_rows), 1)

    def score_tile(q, carry):
        q_tile = qbuf[pl.ds(q * devices_per_tile, devices_per_tile)].reshape(tile_rows, width)
        for b in range(n_blk):
            scores = lax.dot_general(
                kbuf[b], q_tile, (((1,), (1,)), ((), ())), preferred_element_type=jnp.float32
            )
            for kb in range(key_blocks):
                packed = jnp.zeros((words, tile_rows), jnp.int32)
                for j in range(slots):
                    listed = (ids_ref[q, j] == b * key_blocks + kb).astype(jnp.int32)
                    packed = packed + listed * mask_ref[q, j]
                bits = jnp.bitwise_and(
                    jnp.right_shift(
                        jnp.broadcast_to(packed[:, None, :], (words, 8, tile_rows)), shifts
                    ),
                    1,
                ).reshape(tile_rows, tile_rows)
                part = scores[kb * tile_rows:(kb + 1) * tile_rows] * scale
                weight = bits.astype(jnp.float32) * (1.0 / (1.0 + jnp.exp(-part)))
                wbuf[q, pl.ds(b * kv_rows + kb * tile_rows, tile_rows)] = weight.astype(jnp.bfloat16)
        return carry

    lax.fori_loop(0, tiles, score_tile, 0)

    pairs_per_tile = devices_per_tile // n_lo
    r1, r2, r3 = [], [], []

    def produce(c):
        for copy in v_copies[c][1:]:
            copy.wait_recv()
        v_chunk = vbuf[c].reshape(n_blk * kv_rows, cw)
        for q in range(tiles):
            added = lax.dot_general(
                wbuf[q], v_chunk, (((0,), (0,)), ((), ())), preferred_element_type=jnp.float32
            )
            for p in range(pairs_per_tile):
                first = added[(2 * p) * rows:(2 * p + 1) * rows]
                second = added[(2 * p + 1) * rows:(2 * p + 2) * rows]
                pair = q * pairs_per_tile + p
                h, m = pair // n_mid, pair % n_mid
                keep1[c, m, h] = jnp.where(lo == 0, first, second)
                s1_send[c, m, h] = jnp.where(lo == 0, second, first).astype(jnp.bfloat16)
        r1.append(start(remote(s1_send.at[c], s1_recv.at[c], r1_send.at[c], r1_recv.at[c], core_peer)))

    def along_mid(c):
        r1[c].wait_recv()
        s2_send[c] = (
            keep1[c, 1 - mid] + s1_recv[c, 1 - mid].astype(jnp.float32)
        ).astype(jnp.bfloat16)
        r2.append(start(remote(s2_send.at[c], s2_recv.at[c], r2_send.at[c], r2_recv.at[c], mid_peer)))
        keep2[c] = keep1[c, mid] + s1_recv[c, mid].astype(jnp.float32)

    def along_hi(c):
        r2[c].wait_recv()
        copies = [None]
        for s in range(1, n_hi):
            h = lax.rem(hi + s, n_hi)
            s3_send[c, s] = (keep2[c, h] + s2_recv[c, h].astype(jnp.float32)).astype(jnp.bfloat16)
            copies.append(
                start(
                    remote(
                        s3_send.at[c, s], s3_recv.at[c, s],
                        r3_send.at[c, s], r3_recv.at[c, s], hi_to[s],
                    )
                )
            )
        r3.append(copies)

    def finish(c):
        added = keep2[c, hi] + s2_recv[c, hi].astype(jnp.float32)
        for s in range(1, n_hi):
            r3[c][s].wait_recv()
            added = added + s3_recv[c, s].astype(jnp.float32)
        total[:, pl.ds(c * cw, cw)] = added

    for i in range(n_chunk + 3):
        if i < n_chunk:
            produce(i)
        if 0 <= i - 1 < n_chunk:
            along_mid(i - 1)
        if 0 <= i - 2 < n_chunk:
            along_hi(i - 2)
        if 0 <= i - 3 < n_chunk:
            finish(i - 3)

    aggregate = total[...]
    norm = lax.rsqrt(jnp.mean(aggregate * aggregate, axis=-1, keepdims=True) + 1e-06)
    out_ref[...] = (gate_buf[...] * (aggregate * norm)).astype(out_ref.dtype)
    for copy in pending:
        copy.wait_send()


def per_device(n_blk, n_team, queries, keys, values, block_ids, masks, gate_input, w_gate):
    rows, width = queries.shape[1:]
    kv_rows = keys.shape[2]
    tiles, _, _, tile_rows = masks.shape[2:]
    n_lo = 2
    n_mid = 2
    n_hi = n_team // (n_lo * n_mid)
    n_chunk = 4
    cw = width // n_chunk
    bf16, f32 = jnp.bfloat16, jnp.float32
    vmem = pl.BlockSpec(memory_space=pltpu.VMEM)
    anywhere = pl.BlockSpec(memory_space=pl.ANY)
    dma = pltpu.SemaphoreType.DMA
    out = pl.pallas_call(
        functools.partial(kernel, n_blk, n_team, n_lo, n_mid, n_hi, n_chunk),
        out_shape=jax.ShapeDtypeStruct((rows, width), bf16),
        in_specs=[
            pl.BlockSpec(memory_space=pltpu.SMEM), anywhere, anywhere, anywhere, vmem, vmem, vmem,
        ],
        out_specs=vmem,
        scratch_shapes=[
            pltpu.VMEM((n_team, rows, width), bf16),
            pltpu.VMEM((n_blk, kv_rows, width), bf16),
            pltpu.VMEM((n_chunk, n_blk, kv_rows, cw), bf16),
            pltpu.VMEM((tiles, n_blk * kv_rows, tile_rows), bf16),
            pltpu.VMEM((rows, width), f32),
            pltpu.VMEM((rows, width), f32),
            pltpu.VMEM((n_chunk, n_mid, n_hi, rows, cw), f32),
            pltpu.VMEM((n_chunk, n_mid, n_hi, rows, cw), bf16),
            pltpu.VMEM((n_chunk, n_mid, n_hi, rows, cw), bf16),
            pltpu.VMEM((n_chunk, n_hi, rows, cw), f32),
            pltpu.VMEM((n_chunk, n_hi, rows, cw), bf16),
            pltpu.VMEM((n_chunk, n_hi, rows, cw), bf16),
            pltpu.VMEM((n_chunk, n_hi, rows, cw), bf16),
            pltpu.VMEM((n_chunk, n_hi, rows, cw), bf16),
            dma((2 + n_chunk,)),
            dma((1 + n_chunk, n_blk)), dma((1 + n_chunk, n_blk)),
            dma((n_hi,)), dma((n_hi,)),
            dma((n_hi,)), dma((n_hi,)),
            dma((n_mid, n_hi)), dma((n_mid, n_hi)),
            dma((n_chunk,)), dma((n_chunk,)),
            dma((n_chunk,)), dma((n_chunk,)),
            dma((n_chunk, n_hi)), dma((n_chunk, n_hi)),
        ],
        compiler_params=pltpu.CompilerParams(
            collective_id=0, has_side_effects=True, vmem_limit_bytes=40 * 1024 * 1024
        ),
    )(
        block_ids[0, 0], queries[0], keys[0, 0], values[0, 0], masks[0, 0], gate_input[0], w_gate,
    )
    return out[None]


def solution(mesh):
    return jax.shard_map(
        functools.partial(per_device, mesh.shape["blk"], mesh.shape["team"]),
        mesh=mesh,
        in_specs=(
            P("blk", "team", None),
            P("blk", "team", None, None),
            P("blk", "team", None, None),
            P("blk", "team", None, None),
            P("blk", "team", None, None, None, None),
            P("blk", "team", None),
            P(),
        ),
        out_specs=P("blk", "team", None),
        check_vma=False,
    )
```

```python
import functools
import math

import jax
import jax.numpy as jnp
from jax import lax
from jax.experimental import pallas as pl
from jax.experimental.pallas import tpu as pltpu
from jax.sharding import PartitionSpec as P

MESH = pl.DeviceIdType.MESH


def kernel(
    n_blk, n_team, n_lo, n_mid, n_hi, n_chunk,
    ids_hbm, q_ref, k_ref, v_ref, mask_hbm, gate_in_hbm, w_gate_hbm,
    out_ref,
    ids_ref, mask_ref, gate_in_ref, w_gate_ref, qbuf, kbuf, vbuf, wbuf, gate_buf, total,
    keep1, s1_send, s1_recv, keep2, s2_send, s2_recv, s3_send, s3_recv,
    loc_sem,
    kv_send, kv_recv,
    zq_send, zq_recv, yq_send, yq_recv, cq_send, cq_recv,
    r1_send, r1_recv, r2_send, r2_recv, r3_send, r3_recv,
):
    rows, width = q_ref.shape
    kv_rows = k_ref.shape[0]
    tiles, slots, words, tile_rows = mask_ref.shape
    key_blocks = kv_rows // tile_rows
    cw = width // n_chunk
    scale = 1.0 / math.sqrt(width)

    blk = lax.axis_index("blk")
    team = lax.axis_index("team")
    lo = lax.rem(team, n_lo)
    mid = lax.rem(team // n_lo, n_mid)
    hi = team // (n_lo * n_mid)

    def index_of(h, m, l):
        return (h * n_mid + m) * n_lo + l

    core_peer = (blk, index_of(hi, mid, 1 - lo))
    mid_peer = (blk, index_of(hi, 1 - mid, lo))
    hi_to = [(blk, index_of(lax.rem(hi + s, n_hi), mid, lo)) for s in range(n_hi)]
    hi_from = [lax.rem(hi + n_hi - s, n_hi) for s in range(n_hi)]
    blk_to = [(lax.rem(blk + s, n_blk), team) for s in range(n_blk)]
    blk_from = [lax.rem(blk + n_blk - s, n_blk) for s in range(n_blk)]

    def remote(src, dst, send, recv, device):
        return pltpu.make_async_remote_copy(
            src_ref=src, dst_ref=dst, send_sem=send, recv_sem=recv,
            device_id=device, device_id_type=MESH,
        )

    locals_ = [
        pltpu.make_async_copy(q_ref, qbuf.at[team], loc_sem.at[0]),
        pltpu.make_async_copy(k_ref, kbuf.at[blk], loc_sem.at[1]),
    ]
    for c in range(n_chunk):
        locals_.append(
            pltpu.make_async_copy(
                v_ref.at[:, pl.ds(c * cw, cw)], vbuf.at[c, blk], loc_sem.at[2 + c]
            )
        )
    gate_copies = [
        pltpu.make_async_copy(gate_in_hbm, gate_in_ref, loc_sem.at[2 + n_chunk]),
        pltpu.make_async_copy(w_gate_hbm, w_gate_ref, loc_sem.at[3 + n_chunk]),
    ]
    locals_.append(pltpu.make_async_copy(mask_hbm, mask_ref, loc_sem.at[4 + n_chunk]))
    locals_.append(pltpu.make_async_copy(ids_hbm, ids_ref, loc_sem.at[5 + n_chunk]))
    for copy in locals_ + gate_copies:
        copy.start()

    barrier = pltpu.get_barrier_semaphore()
    partners = [core_peer, mid_peer] + hi_to[1:] + blk_to[1:]
    for device in partners:
        pl.semaphore_signal(barrier, inc=1, device_id=device, device_id_type=MESH)
    pl.semaphore_wait(barrier, len(partners))

    pending = []

    def start(copy):
        copy.start()
        pending.append(copy)
        return copy

    def sent(copy):
        copy.wait_send()
        pending[:] = [other for other in pending if other is not copy]

    shifts = lax.broadcasted_iota(jnp.int32, (words, 8, tile_rows), 1)
    devices_per_tile = tile_rows // rows

    def score(q, b):
        q_tile = qbuf[pl.ds(q * devices_per_tile, devices_per_tile)].reshape(tile_rows, width)
        scores = lax.dot_general(
            kbuf[b], q_tile, (((1,), (1,)), ((), ())), preferred_element_type=jnp.float32
        )
        for kb in range(key_blocks):
            packed = jnp.zeros((words, tile_rows), jnp.int32)
            for j in range(slots):
                listed = (ids_ref[j, q] == b * key_blocks + kb).astype(jnp.int32)
                packed = packed + listed * mask_ref[q, j]
            bits = jnp.bitwise_and(
                jnp.right_shift(
                    jnp.broadcast_to(packed[:, None, :], (words, 8, tile_rows)), shifts
                ),
                1,
            ).reshape(tile_rows, tile_rows)
            part = scores[kb * tile_rows:(kb + 1) * tile_rows] * scale
            weight = bits.astype(jnp.float32) * (1.0 / (1.0 + jnp.exp(-part)))
            at = pl.ds(pl.multiple_of(q * tile_rows, tile_rows), tile_rows)
            wbuf[b, at, pl.ds(kb * tile_rows, tile_rows)] = weight.T.astype(jnp.bfloat16)

    own = qbuf.at[team]
    zq = [None] + [
        remote(q_ref, own, zq_send.at[s], zq_recv.at[s], hi_to[s]) for s in range(1, n_hi)
    ]
    kv = [[remote(k_ref, kbuf.at[blk], kv_send.at[0, s], kv_recv.at[0, s], blk_to[s])
           for s in range(1, n_blk)]]
    for c in range(n_chunk):
        kv.append([
            remote(
                v_ref.at[:, pl.ds(c * cw, cw)], vbuf.at[c, blk],
                kv_send.at[1 + c, s], kv_recv.at[1 + c, s], blk_to[s],
            )
            for s in range(1, n_blk)
        ])
    moved = [0]

    def next_kv():
        n = moved[0]
        if n > n_chunk:
            return
        if n > 1:
            for copy in kv[n - 2]:
                sent(copy)
        for copy in kv[n]:
            start(copy)
        moved[0] = n + 1

    for s in range(1, n_hi):
        start(zq[s])
    next_kv()
    yq = [start(remote(q_ref, own, yq_send.at[0], yq_recv.at[0], mid_peer))]
    next_kv()
    cq = [[start(remote(q_ref, own, cq_send.at[0, 0], cq_recv.at[0, 0], core_peer))], []]
    per_tile = devices_per_tile // n_lo

    def onward(s):
        yq[s].wait_recv()
        shard = qbuf.at[index_of(hi_from[s], 1 - mid, lo)]
        cq[1].append(start(remote(shard, shard, cq_send.at[1, s], cq_recv.at[1, s], core_peer)))

    def own_score(m, s):
        cq[m][s].wait_recv()
        if per_tile == 1:
            score(hi_from[s] * n_mid + (mid if m == 0 else 1 - mid), blk)

    for s in range(1, n_hi):
        zq[s].wait_recv()
        shard = qbuf.at[index_of(hi_from[s], mid, lo)]
        yq.append(start(remote(shard, shard, yq_send.at[s], yq_recv.at[s], mid_peer)))
        cq[0].append(start(remote(shard, shard, cq_send.at[0, s], cq_recv.at[0, s], core_peer)))
        onward(s - 1)
        if s == 1:
            for copy in locals_:
                copy.wait()
        own_score(0, s - 1)
    next_kv()
    own_score(0, n_hi - 1)
    for s in range(n_hi - 1):
        own_score(1, s)
    next_kv()
    onward(n_hi - 1)

    for copy in gate_copies:
        copy.wait()
    gate_pre = jnp.dot(gate_in_ref[...], w_gate_ref[...], preferred_element_type=jnp.float32)
    gate_buf[...] = gate_pre / (1.0 + jnp.exp(-gate_pre))

    own_score(1, n_hi - 1)
    next_kv()

    def score_tiles(b):
        def body(q, carry):
            score(q, b)
            return carry
        lax.fori_loop(0, tiles, body, 0, unroll=4)

    if per_tile > 1:
        score_tiles(blk)
    for s in range(1, n_blk):
        kv[0][s - 1].wait_recv()
        score_tiles(blk_from[s])

    r1, r2, r3 = [], [], []

    def produce(c):
        next_kv()
        for copy in kv[1 + c]:
            copy.wait_recv()
        added = jnp.dot(wbuf[0], vbuf[c, 0], preferred_element_type=jnp.float32)
        for b in range(1, n_blk):
            added = added + jnp.dot(wbuf[b], vbuf[c, b], preferred_element_type=jnp.float32)
        for pair in range(n_hi * n_mid):
            first = added[(2 * pair) * rows:(2 * pair + 1) * rows]
            second = added[(2 * pair + 1) * rows:(2 * pair + 2) * rows]
            h, m = pair // n_mid, pair % n_mid
            keep1[c, m, h] = jnp.where(lo == 0, first, second)
            s1_send[c, m, h] = jnp.where(lo == 0, second, first).astype(jnp.bfloat16)
        r1.append(start(remote(s1_send.at[c], s1_recv.at[c], r1_send.at[c], r1_recv.at[c], core_peer)))

    def along_mid(c):
        r1[c].wait_recv()
        s2_send[c] = (
            keep1[c, 1 - mid] + s1_recv[c, 1 - mid].astype(jnp.float32)
        ).astype(jnp.bfloat16)
        r2.append(start(remote(s2_send.at[c], s2_recv.at[c], r2_send.at[c], r2_recv.at[c], mid_peer)))
        keep2[c] = keep1[c, mid] + s1_recv[c, mid].astype(jnp.float32)

    def along_hi(c):
        r2[c].wait_recv()
        copies = [None]
        for s in range(1, n_hi):
            h = lax.rem(hi + s, n_hi)
            s3_send[c, s] = (keep2[c, h] + s2_recv[c, h].astype(jnp.float32)).astype(jnp.bfloat16)
            copies.append(
                start(
                    remote(
                        s3_send.at[c, s], s3_recv.at[c, s],
                        r3_send.at[c, s], r3_recv.at[c, s], hi_to[s],
                    )
                )
            )
        r3.append(copies)

    def finish(c):
        added = keep2[c, hi] + s2_recv[c, hi].astype(jnp.float32)
        for s in range(1, n_hi):
            r3[c][s].wait_recv()
            added = added + s3_recv[c, s].astype(jnp.float32)
        total[:, pl.ds(c * cw, cw)] = added

    for c in range(n_chunk):
        produce(c)
        if c > 0:
            along_mid(c - 1)
    along_mid(n_chunk - 1)
    for stage in (along_hi, finish):
        for c in range(n_chunk):
            stage(c)

    aggregate = total[...]
    norm = lax.rsqrt(jnp.mean(aggregate * aggregate, axis=-1, keepdims=True) + 1e-06)
    out_ref[...] = (gate_buf[...] * (aggregate * norm)).astype(out_ref.dtype)
    for copy in pending:
        copy.wait_send()


def per_device(n_blk, n_team, queries, keys, values, block_ids, masks, gate_input, w_gate):
    rows, width = queries.shape[1:]
    kv_rows = keys.shape[2]
    tiles, slots, words, tile_rows = masks.shape[2:]
    n_lo = 2
    n_mid = 2
    n_hi = n_team // (n_lo * n_mid)
    n_chunk = 4
    cw = width // n_chunk
    bf16, f32 = jnp.bfloat16, jnp.float32
    vmem = pl.BlockSpec(memory_space=pltpu.VMEM)
    hbm = pl.BlockSpec(memory_space=pltpu.HBM)
    dma = pltpu.SemaphoreType.DMA
    out = pl.pallas_call(
        functools.partial(kernel, n_blk, n_team, n_lo, n_mid, n_hi, n_chunk),
        out_shape=jax.ShapeDtypeStruct((rows, width), bf16),
        in_specs=[hbm] * 7,
        out_specs=vmem,
        scratch_shapes=[
            pltpu.SMEM((slots, tiles), jnp.int32),
            pltpu.VMEM((tiles, slots, words, tile_rows), jnp.int32),
            pltpu.VMEM((rows, width), bf16),
            pltpu.VMEM((width, width), bf16),
            pltpu.VMEM((n_team, rows, width), bf16),
            pltpu.VMEM((n_blk, kv_rows, width), bf16),
            pltpu.VMEM((n_chunk, n_blk, kv_rows, cw), bf16),
            pltpu.VMEM((n_blk, tiles * tile_rows, kv_rows), bf16),
            pltpu.VMEM((rows, width), f32),
            pltpu.VMEM((rows, width), f32),
            pltpu.VMEM((n_chunk, n_mid, n_hi, rows, cw), f32),
            pltpu.VMEM((n_chunk, n_mid, n_hi, rows, cw), bf16),
            pltpu.VMEM((n_chunk, n_mid, n_hi, rows, cw), bf16),
            pltpu.VMEM((n_chunk, n_hi, rows, cw), f32),
            pltpu.VMEM((n_chunk, n_hi, rows, cw), bf16),
            pltpu.VMEM((n_chunk, n_hi, rows, cw), bf16),
            pltpu.VMEM((n_chunk, n_hi, rows, cw), bf16),
            pltpu.VMEM((n_chunk, n_hi, rows, cw), bf16),
            dma((6 + n_chunk,)),
            dma((1 + n_chunk, n_blk)), dma((1 + n_chunk, n_blk)),
            dma((n_hi,)), dma((n_hi,)),
            dma((n_hi,)), dma((n_hi,)),
            dma((n_mid, n_hi)), dma((n_mid, n_hi)),
            dma((n_chunk,)), dma((n_chunk,)),
            dma((n_chunk,)), dma((n_chunk,)),
            dma((n_chunk, n_hi)), dma((n_chunk, n_hi)),
        ],
        compiler_params=pltpu.CompilerParams(
            collective_id=0, has_side_effects=True, vmem_limit_bytes=56 * 1024 * 1024
        ),
    )(
        block_ids[0, 0].T, queries[0], keys[0, 0], values[0, 0], masks[0, 0], gate_input[0], w_gate,
    )
    return out[None]


def solution(mesh):
    return jax.shard_map(
        functools.partial(per_device, mesh.shape["blk"], mesh.shape["team"]),
        mesh=mesh,
        in_specs=(
            P("blk", "team", None),
            P("blk", "team", None, None),
            P("blk", "team", None, None),
            P("blk", "team", None, None),
            P("blk", "team", None, None, None, None),
            P("blk", "team", None),
            P(),
        ),
        out_specs=P("blk", "team", None),
        check_vma=False,
    )
```

```python
import functools
import math

import jax
import jax.numpy as jnp
from jax import lax
from jax.experimental import pallas as pl
from jax.experimental.pallas import tpu as pltpu
from jax.sharding import PartitionSpec as P

MESH = pl.DeviceIdType.MESH


def kernel(
    n_blk, n_team, n_lo, n_mid, n_hi, n_chunk,
    ids_hbm, q_ref, k_ref, v_ref, mask_hbm, gate_in_hbm, w_gate_hbm,
    out_ref,
    ids_ref, mask_ref, gate_in_ref, w_gate_ref, qbuf, kbuf, vbuf, wbuf, gate_buf, total,
    keep1, s1_send, s1_recv, keep2, s2_send, s2_recv, s3_send, s3_recv,
    loc_sem,
    kv_send, kv_recv,
    zq_send, zq_recv, yq_send, yq_recv, cq_send, cq_recv,
    r1_send, r1_recv, r2_send, r2_recv, r3_send, r3_recv,
):
    rows, width = q_ref.shape
    kv_rows = k_ref.shape[0]
    tiles, slots, words, tile_rows = mask_ref.shape
    key_blocks = kv_rows // tile_rows
    cw = width // n_chunk
    scale = 1.0 / math.sqrt(width)

    blk = lax.axis_index("blk")
    team = lax.axis_index("team")
    lo = lax.rem(team, n_lo)
    mid = lax.rem(team // n_lo, n_mid)
    hi = team // (n_lo * n_mid)

    def index_of(h, m, l):
        return (h * n_mid + m) * n_lo + l

    core_peer = (blk, index_of(hi, mid, 1 - lo))
    mid_peer = (blk, index_of(hi, 1 - mid, lo))
    hi_to = [(blk, index_of(lax.rem(hi + s, n_hi), mid, lo)) for s in range(n_hi)]
    hi_from = [lax.rem(hi + n_hi - s, n_hi) for s in range(n_hi)]
    blk_to = [(lax.rem(blk + s, n_blk), team) for s in range(n_blk)]
    blk_from = [lax.rem(blk + n_blk - s, n_blk) for s in range(n_blk)]

    def remote(src, dst, send, recv, device):
        return pltpu.make_async_remote_copy(
            src_ref=src, dst_ref=dst, send_sem=send, recv_sem=recv,
            device_id=device, device_id_type=MESH,
        )

    locals_ = [
        pltpu.make_async_copy(q_ref, qbuf.at[team], loc_sem.at[0]),
        pltpu.make_async_copy(k_ref, kbuf.at[blk], loc_sem.at[1]),
    ]
    for c in range(n_chunk):
        locals_.append(
            pltpu.make_async_copy(
                v_ref.at[:, pl.ds(c * cw, cw)], vbuf.at[c, blk], loc_sem.at[2 + c]
            )
        )
    gate_copies = [
        pltpu.make_async_copy(gate_in_hbm, gate_in_ref, loc_sem.at[2 + n_chunk]),
        pltpu.make_async_copy(w_gate_hbm, w_gate_ref, loc_sem.at[3 + n_chunk]),
    ]
    locals_.append(pltpu.make_async_copy(mask_hbm, mask_ref, loc_sem.at[4 + n_chunk]))
    locals_.append(pltpu.make_async_copy(ids_hbm, ids_ref, loc_sem.at[5 + n_chunk]))
    for copy in locals_ + gate_copies:
        copy.start()

    barrier = pltpu.get_barrier_semaphore()
    partners = [core_peer, mid_peer] + hi_to[1:] + blk_to[1:]
    for device in partners:
        pl.semaphore_signal(barrier, inc=1, device_id=device, device_id_type=MESH)
    for copy in gate_copies:
        copy.wait()
    gate_pre = jnp.dot(gate_in_ref[...], w_gate_ref[...], preferred_element_type=jnp.float32)
    gate_buf[...] = gate_pre / (1.0 + jnp.exp(-gate_pre))

    pl.semaphore_wait(barrier, len(partners))

    pending = []

    def start(copy):
        copy.start()
        pending.append(copy)
        return copy

    def sent(copy):
        copy.wait_send()
        pending[:] = [other for other in pending if other is not copy]

    shifts = lax.broadcasted_iota(jnp.int32, (words, 8, tile_rows), 1)
    devices_per_tile = tile_rows // rows

    def score(q, b):
        q_tile = qbuf[pl.ds(q * devices_per_tile, devices_per_tile)].reshape(tile_rows, width)
        scores = lax.dot_general(
            kbuf[b], q_tile, (((1,), (1,)), ((), ())), preferred_element_type=jnp.float32
        )
        for kb in range(key_blocks):
            packed = jnp.zeros((words, tile_rows), jnp.int32)
            for j in range(slots):
                listed = (ids_ref[j, q] == b * key_blocks + kb).astype(jnp.int32)
                packed = packed + listed * mask_ref[q, j]
            bits = jnp.bitwise_and(
                jnp.right_shift(
                    jnp.broadcast_to(packed[:, None, :], (words, 8, tile_rows)), shifts
                ),
                1,
            ).reshape(tile_rows, tile_rows)
            part = scores[kb * tile_rows:(kb + 1) * tile_rows] * scale
            weight = bits.astype(jnp.float32) * (1.0 / (1.0 + jnp.exp(-part)))
            at = pl.ds(pl.multiple_of(q * tile_rows, tile_rows), tile_rows)
            wbuf[b, at, pl.ds(kb * tile_rows, tile_rows)] = weight.T.astype(jnp.bfloat16)

    own = qbuf.at[team]
    zq = [None] + [
        remote(q_ref, own, zq_send.at[s], zq_recv.at[s], hi_to[s]) for s in range(1, n_hi)
    ]
    kv = [[remote(k_ref, kbuf.at[blk], kv_send.at[0, s], kv_recv.at[0, s], blk_to[s])
           for s in range(1, n_blk)]]
    for c in range(n_chunk):
        kv.append([
            remote(
                v_ref.at[:, pl.ds(c * cw, cw)], vbuf.at[c, blk],
                kv_send.at[1 + c, s], kv_recv.at[1 + c, s], blk_to[s],
            )
            for s in range(1, n_blk)
        ])
    moved = [0]

    def next_kv():
        n = moved[0]
        if n > n_chunk:
            return
        if n > 1:
            for copy in kv[n - 2]:
                sent(copy)
        for copy in kv[n]:
            start(copy)
        moved[0] = n + 1

    for s in range(1, n_hi):
        start(zq[s])
    next_kv()
    yq = [start(remote(q_ref, own, yq_send.at[0], yq_recv.at[0], mid_peer))]
    next_kv()
    cq = [[start(remote(q_ref, own, cq_send.at[0, 0], cq_recv.at[0, 0], core_peer))], []]
    per_tile = devices_per_tile // n_lo

    def onward(s):
        yq[s].wait_recv()
        shard = qbuf.at[index_of(hi_from[s], 1 - mid, lo)]
        cq[1].append(start(remote(shard, shard, cq_send.at[1, s], cq_recv.at[1, s], core_peer)))

    def own_score(m, s):
        cq[m][s].wait_recv()
        if per_tile == 1:
            tile = hi_from[s] * n_mid + (mid if m == 0 else 1 - mid)
            score(tile, blk)
            if m == 1:
                for n in range(1, n_blk):
                    score(tile, blk_from[n])

    for s in range(1, n_hi):
        zq[s].wait_recv()
        shard = qbuf.at[index_of(hi_from[s], mid, lo)]
        yq.append(start(remote(shard, shard, yq_send.at[s], yq_recv.at[s], mid_peer)))
        cq[0].append(start(remote(shard, shard, cq_send.at[0, s], cq_recv.at[0, s], core_peer)))
        onward(s - 1)
        if s == 1:
            for copy in locals_:
                copy.wait()
        own_score(0, s - 1)
    next_kv()
    own_score(0, n_hi - 1)
    for n in range(1, n_blk):
        kv[0][n - 1].wait_recv()
        if per_tile == 1:
            for s in range(n_hi):
                score(hi_from[s] * n_mid + mid, blk_from[n])
    for s in range(n_hi - 1):
        own_score(1, s)
    next_kv()
    onward(n_hi - 1)

    own_score(1, n_hi - 1)
    next_kv()

    def score_tiles(b):
        def body(q, carry):
            score(q, b)
            return carry
        lax.fori_loop(0, tiles, body, 0, unroll=4)

    if per_tile > 1:
        for s in range(n_blk):
            score_tiles(blk_from[s])

    r1, r2, r3 = [], [], []

    def produce(c):
        next_kv()
        for copy in kv[1 + c]:
            copy.wait_recv()
        added = jnp.dot(wbuf[0], vbuf[c, 0], preferred_element_type=jnp.float32)
        for b in range(1, n_blk):
            added = added + jnp.dot(wbuf[b], vbuf[c, b], preferred_element_type=jnp.float32)
        for pair in range(n_hi * n_mid):
            first = added[(2 * pair) * rows:(2 * pair + 1) * rows]
            second = added[(2 * pair + 1) * rows:(2 * pair + 2) * rows]
            h, m = pair // n_mid, pair % n_mid
            keep1[c, m, h] = jnp.where(lo == 0, first, second)
            s1_send[c, m, h] = jnp.where(lo == 0, second, first).astype(jnp.bfloat16)
        r1.append(start(remote(s1_send.at[c], s1_recv.at[c], r1_send.at[c], r1_recv.at[c], core_peer)))

    def along_mid(c):
        r1[c].wait_recv()
        s2_send[c] = (
            keep1[c, 1 - mid] + s1_recv[c, 1 - mid].astype(jnp.float32)
        ).astype(jnp.bfloat16)
        r2.append(start(remote(s2_send.at[c], s2_recv.at[c], r2_send.at[c], r2_recv.at[c], mid_peer)))
        keep2[c] = keep1[c, mid] + s1_recv[c, mid].astype(jnp.float32)

    def along_hi(c):
        r2[c].wait_recv()
        copies = [None]
        for s in range(1, n_hi):
            h = lax.rem(hi + s, n_hi)
            s3_send[c, s] = (keep2[c, h] + s2_recv[c, h].astype(jnp.float32)).astype(jnp.bfloat16)
            copies.append(
                start(
                    remote(
                        s3_send.at[c, s], s3_recv.at[c, s],
                        r3_send.at[c, s], r3_recv.at[c, s], hi_to[s],
                    )
                )
            )
        r3.append(copies)

    def finish(c):
        added = keep2[c, hi] + s2_recv[c, hi].astype(jnp.float32)
        for s in range(1, n_hi):
            r3[c][s].wait_recv()
            added = added + s3_recv[c, s].astype(jnp.float32)
        total[:, pl.ds(c * cw, cw)] = added

    for c in range(n_chunk):
        produce(c)
        if c > 0:
            along_mid(c - 1)
    along_mid(n_chunk - 1)
    for stage in (along_hi, finish):
        for c in range(n_chunk):
            stage(c)

    aggregate = total[...]
    norm = lax.rsqrt(jnp.mean(aggregate * aggregate, axis=-1, keepdims=True) + 1e-06)
    out_ref[...] = (gate_buf[...] * (aggregate * norm)).astype(out_ref.dtype)
    for copy in pending:
        copy.wait_send()


def per_device(n_blk, n_team, queries, keys, values, block_ids, masks, gate_input, w_gate):
    rows, width = queries.shape[1:]
    kv_rows = keys.shape[2]
    tiles, slots, words, tile_rows = masks.shape[2:]
    n_lo = 2
    n_mid = 2
    n_hi = n_team // (n_lo * n_mid)
    n_chunk = 4
    cw = width // n_chunk
    bf16, f32 = jnp.bfloat16, jnp.float32
    vmem = pl.BlockSpec(memory_space=pltpu.VMEM)
    hbm = pl.BlockSpec(memory_space=pltpu.HBM)
    dma = pltpu.SemaphoreType.DMA
    out = pl.pallas_call(
        functools.partial(kernel, n_blk, n_team, n_lo, n_mid, n_hi, n_chunk),
        out_shape=jax.ShapeDtypeStruct((rows, width), bf16),
        in_specs=[hbm] * 7,
        out_specs=vmem,
        scratch_shapes=[
            pltpu.SMEM((slots, tiles), jnp.int32),
            pltpu.VMEM((tiles, slots, words, tile_rows), jnp.int32),
            pltpu.VMEM((rows, width), bf16),
            pltpu.VMEM((width, width), bf16),
            pltpu.VMEM((n_team, rows, width), bf16),
            pltpu.VMEM((n_blk, kv_rows, width), bf16),
            pltpu.VMEM((n_chunk, n_blk, kv_rows, cw), bf16),
            pltpu.VMEM((n_blk, tiles * tile_rows, kv_rows), bf16),
            pltpu.VMEM((rows, width), f32),
            pltpu.VMEM((rows, width), f32),
            pltpu.VMEM((n_chunk, n_mid, n_hi, rows, cw), f32),
            pltpu.VMEM((n_chunk, n_mid, n_hi, rows, cw), bf16),
            pltpu.VMEM((n_chunk, n_mid, n_hi, rows, cw), bf16),
            pltpu.VMEM((n_chunk, n_hi, rows, cw), f32),
            pltpu.VMEM((n_chunk, n_hi, rows, cw), bf16),
            pltpu.VMEM((n_chunk, n_hi, rows, cw), bf16),
            pltpu.VMEM((n_chunk, n_hi, rows, cw), bf16),
            pltpu.VMEM((n_chunk, n_hi, rows, cw), bf16),
            dma((6 + n_chunk,)),
            dma((1 + n_chunk, n_blk)), dma((1 + n_chunk, n_blk)),
            dma((n_hi,)), dma((n_hi,)),
            dma((n_hi,)), dma((n_hi,)),
            dma((n_mid, n_hi)), dma((n_mid, n_hi)),
            dma((n_chunk,)), dma((n_chunk,)),
            dma((n_chunk,)), dma((n_chunk,)),
            dma((n_chunk, n_hi)), dma((n_chunk, n_hi)),
        ],
        compiler_params=pltpu.CompilerParams(
            collective_id=0, has_side_effects=True, vmem_limit_bytes=56 * 1024 * 1024
        ),
    )(
        block_ids[0, 0].T, queries[0], keys[0, 0], values[0, 0], masks[0, 0], gate_input[0], w_gate,
    )
    return out[None]


def solution(mesh):
    return jax.shard_map(
        functools.partial(per_device, mesh.shape["blk"], mesh.shape["team"]),
        mesh=mesh,
        in_specs=(
            P("blk", "team", None),
            P("blk", "team", None, None),
            P("blk", "team", None, None),
            P("blk", "team", None, None),
            P("blk", "team", None, None, None, None),
            P("blk", "team", None),
            P(),
        ),
        out_specs=P("blk", "team", None),
        check_vma=False,
    )
```
